32 devices in a mesh: band: 4 (over y, x), sector: 8 (over z, core).
Axes of the slice: x: 2, y: 2, z: 4, core: 2. Of those that a mesh axis runs over, the one named last changes fastest.
Arguments:
- grid_cells: bfloat16 [2048, 128, 128], P(('band', 'sector')), may hold values from -6 to 6
- remap_weight: bfloat16 [2048, 2, 128, 128], P(('band', 'sector')), may hold values from -0.15625 to 0.15625
- remap_dest: int32 [2048, 2], P(('band', 'sector')), may hold values from 0 to 31, all different within a row; in each aligned block of 64 rows (0 to 63, 64 to 127, ...) at most 8 rows name the same one
- remap_tile: int32 [2048, 2], P(('band', 'sector')), may hold values from 0 to 11
- w_embed: bfloat16 [128, 1024], replicated, may hold values from -0.5 to 0.5
- norm_gain: float32 [1024], replicated, may hold values from 0.25 to 1.75
- w_query: bfloat16 [1024, 1024], replicated
- w_key: bfloat16 [1024, 1024], replicated
- w_value: bfloat16 [1024, 1024], replicated, may hold values from -0.1875 to 0.1875
- w_out: bfloat16 [1024, 1024], replicated, may hold values from -0.1875 to 0.1875
- neighbours: int32 [8, 48, 9], P('band', 'sector'), may hold values from 0 to 383, as said below
Outputs:
- layer_out: bfloat16 [8, 48, 128, 1024], P('band', 'sector')
The draws below stay inside these ranges and needn't reach their ends.
Inputs may be any that keep to these rules, and one draw needn't show every extreme that they name: `remap_dest`: within the row-blocks of one device, no device number is named more than 8 times; some number is named exactly 8 times. `neighbours`: entry 0 of a tile is the tile itself; every entry lies at most one tile row and one tile column away, columns counted around the sphere, rows never past the first or last; entries may repeat.
All inputs are finite; a program needn't handle non-finite values.
Results may differ from the reference program's by a relative error of at most 0.0064.
Values may be sent and summed in bfloat16 or wider, within the bound.
No kernel may reach another device: no remote copies, remote signals or barrier semaphores. Data moves between devices by JAX's collectives and lax.ppermute only.
A program may use at most 256 MiB of HBM per device.

```python
import math
import jax
import jax.numpy as jnp
import numpy as np
from jax import lax

D = 1024
HEADS = 16
HD = 64
C_IN = 128
TILE = 128
ROWCELLS = 128
TOP = 2
RB_DEV = 64
TR_DEV = 2
TC_DEV = 6
CAP = 8
ROWBLOCKS = 2048
TROWS = 8
TCOLS = 48
N_SECTOR = 8
DEVICES = 32


def query_key_pair(key):
    shared = jax.random.normal(jax.random.fold_in(key, 101), (D, D), jnp.float32) / math.sqrt(D)
    other = jax.random.normal(jax.random.fold_in(key, 202), (D, D), jnp.float32) / math.sqrt(D)
    return (other, shared)


def draw_w_query(key, part):
    return query_key_pair(key)[0].astype(jnp.bfloat16)


def draw_w_key(key, part):
    return query_key_pair(key)[1].astype(jnp.bfloat16)


def draw_neighbours(key, part):
    shape = (TROWS, TCOLS, 9)
    row_step = jax.random.randint(jax.random.fold_in(key, 303), shape, -1, 2)
    col_step = jax.random.randint(jax.random.fold_in(key, 404), shape, -1, 2)
    first = jnp.arange(9)[None, None, :] == 0
    row_step = jnp.where(first, 0, row_step)
    col_step = jnp.where(first, 0, col_step)
    rows = jnp.arange(TROWS)[:, None, None] + row_step
    cols = jnp.arange(TCOLS)[None, :, None] + col_step
    rows = jnp.clip(rows, 0, TROWS - 1)
    cols = jnp.mod(cols, TCOLS)
    return (rows * TCOLS + cols).astype(jnp.int32)


def place_ends(values, rng, least, top_value):
    shape = values.shape
    spot = [jax.random.randint(jax.random.fold_in(rng, axis), (), 0, shape[axis]) for axis in range(len(shape))]
    values = values.at[tuple(spot)].set(least)
    longest = shape.index(max(shape))
    spot[longest] = (spot[longest] + 1) % shape[longest]
    return values.at[tuple(spot)].set(top_value)


def shard_levels(rng, shape, split, smallest, largest):
    level, own = 1.0, jax.random.fold_in(rng, 6)
    for axis_at, shards_of in split:
        steps = jnp.exp(jax.random.uniform(jax.random.fold_in(own, axis_at), (shards_of,), jnp.float32, smallest / len(split), largest / len(split)))
        level = level * jnp.repeat(steps, shape[axis_at] // shards_of).reshape([-1 if axis == axis_at else 1 for axis in range(len(shape))])
    return level


def deal_out(rng, own, number, rows, count, top, limit, lean):
    ranking = jax.random.permutation(rng, count)
    heavy_load, usual = portions_of(count, rows * top, limit, lean, True), portions_of(count, rows * top, limit, lean, False)
    places = jnp.arange(count)

    def named(sizes, rotation):
        used = int((sizes > 0).sum())
        fixed = max(1, used // 4)
        passed = fixed + (places - fixed + rotation * (used - fixed)) % max(1, count - fixed)
        return jnp.zeros((count,), jnp.int32).at[ranking[jnp.where(places < fixed, places, passed)]].set(jnp.asarray(sizes, jnp.int32))

    sizes = jnp.where(number % 4 == 0, named(heavy_load, number // 4), named(usual, number - number // 4 - 1))
    mixed = jax.random.permutation(jax.random.fold_in(own, 3), count)
    giver, sink = mixed[0:count // 2 * 2:2], mixed[1:count // 2 * 2:2]
    slack = jnp.minimum(sizes[giver] - 1, limit - sizes[sink]) // 2
    slack = jnp.where((giver == ranking[0]) | (sink == ranking[0]) | (sizes[sink] == 0), 0, jnp.maximum(slack, 0))
    passed = jax.random.randint(jax.random.fold_in(own, 4), (count // 2,), 0, 1 << 20) % (slack + 1)
    sizes = sizes.at[giver].add(-passed).at[sink].add(passed)
    labels = jnp.searchsorted(jnp.cumsum(sizes), jnp.arange(rows * top), side="right").astype(jnp.int32)
    listing = labels.reshape(top, rows).T
    listing = listing[jax.random.permutation(jax.random.fold_in(own, 1), rows)]
    rotation = jax.random.randint(jax.random.fold_in(own, 2), (rows, 1), 0, top)
    return jnp.take_along_axis(listing, (jnp.arange(top)[None, :] + rotation) % top, axis=1)


def portions_of(number_of, total, most, skew, full):
    weights = [(1 << 20) // math.isqrt(standing ** skew) + 1 for standing in range(1, number_of + 1)]
    largest = most if full else min(most, max(-(-total // number_of), total * weights[0] // sum(weights)))
    least = 1 if total - largest >= number_of - 1 else 0
    holding, rest = [largest] + [least] * (number_of - 1), total - largest - least * (number_of - 1)
    while rest > 0:
        candidates = [i for i in range(1, number_of) if holding[i] < largest] or [i for i in range(1, number_of) if holding[i] < most]
        pool, remaining = sum([weights[i] for i in candidates]), rest
        for i in candidates:
            extra = min(most - holding[i], max(1, remaining * weights[i] // pool), rest)
            holding[i] = holding[i] + extra
            rest = rest - extra
    return np.array(holding)


def gaussian(rng, shape, spread, most, pieces=(), held_as=jnp.bfloat16):
    loudness = shard_levels(rng, shape, pieces, -0.22, 0.18) if pieces else 1.0
    values = jax.random.normal(rng, shape, jnp.float32) * spread * loudness
    return jnp.minimum(jnp.maximum(values, -most), most).astype(held_as)


def setup_inputs(seed: int = 0) -> dict:
    streams_of = jax.random.split(jax.random.key(seed), 12)
    grid_cells = gaussian(streams_of[0], (ROWBLOCKS, ROWCELLS, C_IN), 1.0, 6.0, ((0, 32),))
    remap_weight = gaussian(streams_of[1], (ROWBLOCKS, TOP, ROWCELLS, TILE), (ROWCELLS * RB_DEV * TOP // (TR_DEV * TC_DEV)) ** -0.5, 0.15625, ((0, 32),))
    remap_dest_keys = jax.random.split(jax.random.fold_in(streams_of[2], 1), ROWBLOCKS // RB_DEV)
    remap_dest_turns = jax.random.permutation(jax.random.fold_in(streams_of[2], 3), ROWBLOCKS // RB_DEV)
    remap_dest = jax.vmap(lambda own, number: deal_out(jax.random.fold_in(streams_of[2], 2), own, number, RB_DEV, DEVICES, TOP, CAP, 2))(remap_dest_keys, remap_dest_turns).reshape((ROWBLOCKS, TOP))
    remap_tile = place_ends(jax.random.randint(streams_of[3], (ROWBLOCKS, TOP), 0, TR_DEV * TC_DEV), jax.random.fold_in(streams_of[3], 1), 0, (TR_DEV * TC_DEV) - 1).astype(jnp.int32)
    w_embed = gaussian(streams_of[4], (C_IN, D), C_IN ** -0.5, 0.5)
    norm_gain = jnp.clip(1.0 + 0.15 * jax.random.normal(streams_of[5], (D,), jnp.float32), 0.25, 1.75)
    w_query = draw_w_query(jax.random.fold_in(streams_of[11], 71), 0)
    w_key = draw_w_key(jax.random.fold_in(streams_of[11], 71), 0)
    w_value = gaussian(streams_of[8], (D, D), D ** -0.5, 0.1875)
    w_out = gaussian(streams_of[9], (D, D), D ** -0.5, 0.1875)
    neighbours = draw_neighbours(jax.random.fold_in(streams_of[11], 71), 0)
    return dict(grid_cells=grid_cells, remap_weight=remap_weight, remap_dest=remap_dest, remap_tile=remap_tile, w_embed=w_embed, norm_gain=norm_gain, w_query=w_query, w_key=w_key, w_value=w_value, w_out=w_out, neighbours=neighbours)


def tile_angles(rows, cols, nrows, ncols, tile):
    place = jnp.arange(tile)
    across = (place // 16).astype(jnp.float32)
    along = (place % 16).astype(jnp.float32)
    theta = math.pi * (rows[..., None].astype(jnp.float32) + (across + 0.5) * 16.0 / tile) / nrows
    phi = 2.0 * math.pi * (cols[..., None].astype(jnp.float32) + (along + 0.5) / 16.0) / ncols
    return jnp.stack([theta, phi], axis=-2)

def rotate(values, angles):
    size = values.shape[-1]
    quarter = size // 4
    freq = jnp.arange(1, quarter + 1).astype(jnp.float32)
    theta = angles[..., 0, :][..., :, None, None] * freq
    phi = angles[..., 1, :][..., :, None, None] * freq

    def turn(pairs, angle):
        lower = pairs[..., :quarter]
        upper = pairs[..., quarter:]
        cosine = jnp.cos(angle)
        sine = jnp.sin(angle)
        return jnp.concatenate([lower * cosine - upper * sine, lower * sine + upper * cosine], axis=-1)
    return jnp.concatenate([turn(values[..., :2 * quarter], theta), turn(values[..., 2 * quarter:], phi)], axis=-1)

def reference(grid_cells, remap_weight, remap_dest, remap_tile, w_embed, norm_gain, w_query, w_key, w_value, w_out, neighbours):
    ntile = TROWS * TCOLS
    dest = remap_dest.reshape(-1)
    local = remap_tile.reshape(-1)
    grow = dest // N_SECTOR * TR_DEV + local // TC_DEV
    gcol = dest % N_SECTOR * TC_DEV + local % TC_DEV
    target = (grow * TCOLS + gcol).astype(jnp.int32).reshape(DEVICES, RB_DEV * TOP)
    cells = grid_cells.reshape(DEVICES, RB_DEV, ROWCELLS, C_IN)
    weights = remap_weight.reshape(DEVICES, RB_DEV, TOP, ROWCELLS, TILE)

    def add_block(total, inputs):
        cell, weight, where = inputs
        part = jnp.einsum('rkct,rcf->rktf', weight.astype(jnp.float32), cell.astype(jnp.float32)).astype(jnp.bfloat16)
        part = lax.optimization_barrier(part).astype(jnp.float32)
        return (total.at[where].add(part.reshape(-1, TILE, C_IN)), None)
    total, _ = lax.scan(add_block, jnp.zeros((ntile, TILE, C_IN), jnp.float32), (cells, weights, target))
    remapped = total.astype(jnp.bfloat16).reshape(-1, C_IN)
    embedded = jnp.dot(remapped, w_embed, preferred_element_type=jnp.float32)
    meansq = lax.optimization_barrier(jnp.mean(embedded * embedded, axis=-1, keepdims=True))
    normed = (embedded * lax.rsqrt(meansq + 1e-05) * norm_gain).astype(jnp.bfloat16)
    rows = jnp.repeat(jnp.arange(TROWS), TCOLS)
    cols = jnp.tile(jnp.arange(TCOLS), TROWS)
    angles = tile_angles(rows, cols, TROWS, TCOLS, TILE)
    queries = rotate(jnp.dot(normed, w_query, preferred_element_type=jnp.float32).reshape(ntile, TILE, HEADS, HD), angles).astype(jnp.bfloat16)
    keys = rotate(jnp.dot(normed, w_key, preferred_element_type=jnp.float32).reshape(ntile, TILE, HEADS, HD), angles).astype(jnp.bfloat16)
    values = jnp.dot(normed, w_value, preferred_element_type=jnp.float32).astype(jnp.bfloat16).reshape(ntile, TILE, HEADS, HD)
    table = neighbours.reshape(ntile, 9)

    def one_tile(inputs):
        query, listed = inputs
        near_keys = keys[listed].reshape(9 * TILE, HEADS, HD)
        near_values = values[listed].reshape(9 * TILE, HEADS, HD)
        scores = jnp.einsum('qhd,khd->hqk', query.astype(jnp.float32), near_keys.astype(jnp.float32)) / math.sqrt(HD)
        probs = jax.nn.softmax(scores, axis=-1).astype(jnp.bfloat16)
        mixed = jnp.einsum('hqk,khd->qhd', probs.astype(jnp.float32), near_values.astype(jnp.float32))
        return mixed.astype(jnp.bfloat16).reshape(TILE, D)
    attended = lax.map(one_tile, (queries, table)).reshape(-1, D)
    result = jnp.dot(attended, w_out, preferred_element_type=jnp.float32) + embedded
    return result.astype(jnp.bfloat16).reshape(TROWS, TCOLS, TILE, D)
```

```python
import functools
import math

import jax
import jax.numpy as jnp
from jax import lax
from jax.experimental import pallas as pl
from jax.experimental.pallas import tpu as pltpu
from jax.sharding import PartitionSpec as P

HEADS = 16
HD = 64
GROUP = 4
NGROUP = HEADS // GROUP
GW = GROUP * HD
QUARTER = HD // 4
LISTED = 9
PAIRS = (LISTED + 1) // 2


def padded(block, sides, width, periodic):
    for axis, dim in sides:
        count = lax.axis_size(axis)
        forward = [(i, i + 1) for i in range(count - 1)]
        if periodic:
            forward.append((count - 1, 0))
        backward = [(target, source) for source, target in forward]
        low = lax.ppermute(
            lax.slice_in_dim(block, block.shape[dim] - width, None, axis=dim), axis, forward
        )
        high = lax.ppermute(lax.slice_in_dim(block, 0, width, axis=dim), axis, backward)
        block = jnp.concatenate([low, block, high], axis=dim)
    return block


def rotary_tables(ext_rows, ext_cols, nrows, ncols, tile):
    place = jnp.arange(tile)
    across = (place // 16).astype(jnp.float32)
    along = (place % 16).astype(jnp.float32)
    theta = math.pi * (ext_rows[:, None].astype(jnp.float32) + (across + 0.5) * 16.0 / tile) / nrows
    phi = 2.0 * math.pi * (ext_cols[:, None].astype(jnp.float32) + (along + 0.5) / 16.0) / ncols
    lane = jnp.arange(GROUP * 2 * QUARTER)
    freq = (lane % QUARTER + 1).astype(jnp.float32)
    lon = (lane // QUARTER) % 2 == 1
    lat_angle = theta[:, :, None] * freq
    lon_angle = phi[:, :, None] * freq
    return (
        jnp.where(lon, 0.0, jnp.cos(lat_angle)),
        jnp.where(lon, 0.0, jnp.sin(lat_angle)),
        jnp.where(lon, jnp.cos(lon_angle), 0.0),
        jnp.where(lon, jnp.sin(lon_angle), 0.0),
    )


def pair_order():
    new = jnp.arange(GW)
    second = new // (GW // 2)
    rest = new % (GW // 2)
    old = rest // (2 * QUARTER) * HD + (rest // QUARTER) % 2 * 2 * QUARTER + second * QUARTER
    old = old + rest % QUARTER
    return (jnp.arange(GW)[:, None] == old[None, :]).astype(jnp.bfloat16)


def window_kernel(
    sel,
    cnt,
    npair,
    ext,
    lat_cos,
    lat_sin,
    lon_cos,
    lon_sin,
    gain,
    w_embed,
    w_query,
    w_key,
    w_value,
    w_out,
    order,
    out,
    keys,
    values,
    queries,
    embedded,
    wq_pairs,
    wk_pairs,
    normed,
    attended,
):
    row = pl.program_id(0)
    erows, ecols, tile, chan = ext.shape
    tcols = ecols - 2
    width = w_embed.shape[1]
    f32 = jnp.float32
    bf16 = jnp.bfloat16

    def project_row(r, own):
        for c in range(0, ecols, 2):
            x = ext[r, c : c + 2].reshape(2 * tile, chan)
            emb = jnp.dot(x, w_embed[...], preferred_element_type=f32)
            meansq = jnp.mean(emb * emb, axis=-1, keepdims=True)
            scaled = emb * lax.rsqrt(meansq + 1e-05) * gain[...]
            normed[c * tile : (c + 2) * tile, :] = scaled.astype(bf16)
            if own:
                for k in range(2):
                    if 1 <= c + k <= tcols:
                        embedded[r - 1, c + k - 1] = emb[k * tile : (k + 1) * tile]

        def turn(full, c):
            cosine = lat_cos[r] + lon_cos[c]
            sine = lat_sin[r] + lon_sin[c]
            lower = full[:, : GW // 2]
            upper = full[:, GW // 2 :]
            return jnp.concatenate(
                [lower * cosine - upper * sine, lower * sine + upper * cosine], axis=1
            )

        def one_group(g, _):
            full = jnp.dot(normed[...], wk_pairs[g], preferred_element_type=f32)
            for c in range(ecols):
                keys[r * ecols + c, g] = turn(full[c * tile : (c + 1) * tile], c).astype(bf16)
            full = jnp.dot(normed[...], w_value[g], preferred_element_type=f32)
            for c in range(ecols):
                values[r * ecols + c, g] = full[c * tile : (c + 1) * tile].astype(bf16)
            if own:
                full = jnp.dot(
                    normed[tile : (tcols + 1) * tile, :], wq_pairs[g], preferred_element_type=f32
                )
                for c in range(tcols):
                    turned = turn(full[c * tile : (c + 1) * tile], c + 1)
                    queries[(r - 1) * tcols + c, g] = (
                        turned * (math.log2(math.e) / math.sqrt(HD))
                    ).astype(bf16)
            return 0

        lax.fori_loop(0, NGROUP, one_group, 0)

    @pl.when(row == 0)
    def _():
        for g in range(NGROUP):
            wq_pairs[g] = jnp.dot(w_query[g], order[...], preferred_element_type=f32).astype(bf16)
            wk_pairs[g] = jnp.dot(w_key[g], order[...], preferred_element_type=f32).astype(bf16)
        project_row(0, False)

        def own_row(r, _):
            project_row(r, True)
            return 0

        lax.fori_loop(1, erows - 1, own_row, 0)
        project_row(erows - 1, False)

    lane = lax.broadcasted_iota(jnp.int32, (tile, GW), 1)
    pair_head = lane % (GW // 2) // (2 * QUARTER)
    value_head = lane // HD

    def one_tile(c, _):
        t = row * tcols + c

        def with_pairs(count):
            def one_group(g, _):
                query = queries[t, g]
                stacked = jnp.concatenate(
                    [jnp.where(pair_head == h, query, jnp.zeros_like(query)) for h in range(GROUP)],
                    axis=0,
                )
                scores = []
                for j in range(count):
                    near = jnp.concatenate(
                        [keys[sel[t, 2 * j], g], keys[sel[t, 2 * j + 1], g]], axis=0
                    )
                    scores.append(
                        lax.dot_general(
                            stacked, near, (((1,), (1,)), ((), ())), preferred_element_type=f32
                        )
                    )
                top = functools.reduce(jnp.maximum, scores)
                top = jnp.max(top, axis=1, keepdims=True)
                total = jnp.zeros((GROUP * tile, tile), f32)
                mixed = jnp.zeros((GROUP * tile, GW), f32)
                for j in range(count):
                    probs = jnp.exp2(scores[j] - top)
                    first = probs[:, :tile] * cnt[t, 2 * j]
                    second = probs[:, tile:] * cnt[t, 2 * j + 1]
                    total = total + (first + second)
                    near = jnp.concatenate(
                        [values[sel[t, 2 * j], g], values[sel[t, 2 * j + 1], g]], axis=0
                    )
                    mixed = mixed + jnp.dot(
                        jnp.concatenate([first, second], axis=1).astype(bf16),
                        near,
                        preferred_element_type=f32,
                    )
                mixed = mixed / jnp.sum(total, axis=1, keepdims=True)
                result = mixed[:tile]
                for h in range(1, GROUP):
                    result = jnp.where(value_head == h, mixed[h * tile : (h + 1) * tile], result)
                attended[g, pl.ds(pl.multiple_of(c * tile, tile), tile), :] = result.astype(bf16)
                return 0

            lax.fori_loop(0, NGROUP, one_group, 0)

        for count in range(1, PAIRS + 1):
            pl.when(npair[t] == count)(functools.partial(with_pairs, count))
        return 0

    lax.fori_loop(0, tcols, one_tile, 0)
    for c in range(0, tcols, 2):
        rows = slice(c * tile, (c + 2) * tile)
        together = jnp.concatenate([attended[g, rows, :] for g in range(NGROUP)], axis=1)
        result = jnp.dot(together, w_out[...], preferred_element_type=f32)
        result = result + embedded[row, c : c + 2].reshape(2 * tile, width)
        out[0, c : c + 2] = result.astype(bf16).reshape(2, tile, width)


def whole(shape):
    return pl.BlockSpec(shape, lambda *_: (0,) * len(shape), pipeline_mode=pl.Buffered(1))


def window(sel, cnt, npair, operands, trows, tcols):
    ext = operands[0]
    erows, ecols, tile, chan = ext.shape
    width = operands[6].shape[1]
    owned = trows * tcols
    bf16 = jnp.bfloat16
    return pl.pallas_call(
        window_kernel,
        out_shape=jax.ShapeDtypeStruct((trows, tcols, tile, width), bf16),
        grid_spec=pltpu.PrefetchScalarGridSpec(
            num_scalar_prefetch=3,
            grid=(trows,),
            in_specs=[whole(x.shape) for x in operands],
            out_specs=pl.BlockSpec((1, tcols, tile, width), lambda r, *_: (r, 0, 0, 0)),
            scratch_shapes=[
                pltpu.VMEM((erows * ecols, NGROUP, tile, GW), bf16),
                pltpu.VMEM((erows * ecols, NGROUP, tile, GW), bf16),
                pltpu.VMEM((owned, NGROUP, tile, GW), bf16),
                pltpu.VMEM((trows, tcols, tile, width), jnp.float32),
                pltpu.VMEM((NGROUP, width, GW), bf16),
                pltpu.VMEM((NGROUP, width, GW), bf16),
                pltpu.VMEM((ecols * tile, width), bf16),
                pltpu.VMEM((NGROUP, tcols * tile, GW), bf16),
            ],
        ),
        compiler_params=pltpu.CompilerParams(vmem_limit_bytes=62 * 1024 * 1024),
    )(sel, cnt, npair, *operands)


def distinct_tiles(index):
    same = index[:, :, None] == index[:, None, :]
    times = jnp.sum(same, axis=2)
    order = jnp.arange(LISTED)
    new = ~jnp.any(same & (order[None, None, :] < order[None, :, None]), axis=2)
    place = jnp.sum(new[:, None, :] & (order[None, None, :] < order[None, :, None]), axis=2)
    slots = jnp.arange(2 * PAIRS)
    put = new[:, :, None] & (place[:, :, None] == slots[None, None, :])
    found = jnp.any(put, axis=1)
    sel = jnp.where(found, jnp.sum(jnp.where(put, index[:, :, None], 0), axis=1), index[:, :1])
    cnt = jnp.sum(jnp.where(put, times[:, :, None], 0), axis=1).astype(jnp.float32)
    npair = (jnp.sum(new, axis=1) + 1) // 2
    return sel.astype(jnp.int32), cnt, npair.astype(jnp.int32)


def by_group(weight):
    return jnp.swapaxes(weight.reshape(weight.shape[0], NGROUP, GW), 0, 1)


def body(
    grid_cells,
    remap_weight,
    remap_dest,
    remap_tile,
    w_embed,
    norm_gain,
    w_query,
    w_key,
    w_value,
    w_out,
    neighbours,
):
    nband = lax.axis_size("band")
    nsect = lax.axis_size("sector")
    ndev = nband * nsect
    blocks, top, rowcells, tile = remap_weight.shape
    chan = grid_cells.shape[2]
    trows, tcols = (neighbours.shape[0], neighbours.shape[1])
    cap = max(2, 2 * blocks * top // ndev)
    items = blocks * top
    parts = jnp.einsum(
        "rkct,rcf->rktf", remap_weight, grid_cells, preferred_element_type=jnp.float32
    )
    parts = parts.astype(jnp.bfloat16).reshape(items, tile, chan)
    dest = remap_dest.reshape(-1)
    local = remap_tile.reshape(-1)
    order = jnp.arange(items)
    earlier = (dest[:, None] == dest[None, :]) & (order[None, :] < order[:, None])
    rank = jnp.sum(earlier.astype(jnp.int32), axis=1)
    slot = dest * cap + rank
    send_parts = jnp.zeros((ndev * cap, tile, chan), jnp.bfloat16).at[slot].set(parts)
    send_ids = jnp.full((ndev * cap,), -1, jnp.int32).at[slot].set(local)
    got_parts, got_ids = (
        lax.all_to_all(send_parts, ("band", "sector"), split_axis=0, concat_axis=0, tiled=True),
        lax.all_to_all(send_ids, ("band", "sector"), split_axis=0, concat_axis=0, tiled=True),
    )
    owned = trows * tcols
    select = (got_ids[None, :] == jnp.arange(owned)[:, None]).astype(jnp.bfloat16)
    remapped = jnp.einsum(
        "ls,stc->ltc", select, got_parts, preferred_element_type=jnp.float32
    ).astype(jnp.bfloat16)
    band_at = lax.axis_index("band")
    sect_at = lax.axis_index("sector")
    nrows = trows * nband
    ncols = tcols * nsect
    ext = padded(remapped.reshape(trows, tcols, tile, chan), (("band", 0),), 1, False)
    ext = padded(ext, (("sector", 1),), 1, True)
    ext_rows = band_at * trows - 1 + jnp.arange(trows + 2)
    ext_cols = jnp.mod(sect_at * tcols - 1 + jnp.arange(tcols + 2), ncols)
    tables = rotary_tables(ext_rows, ext_cols, nrows, ncols, tile)
    local_row = neighbours // ncols - band_at * trows + 1
    local_col = jnp.mod(neighbours % ncols - sect_at * tcols + 1, ncols)
    index = (local_row * (tcols + 2) + local_col).reshape(owned, LISTED)
    sel, cnt, npair = distinct_tiles(index)
    operands = (ext, *tables, norm_gain.reshape(1, -1), w_embed)
    operands += (by_group(w_query), by_group(w_key), by_group(w_value), w_out, pair_order())
    return window(sel, cnt, npair, operands, trows, tcols)


def solution(mesh):
    return jax.shard_map(
        body,
        mesh=mesh,
        in_specs=(
            P(("band", "sector"), None, None),
            P(("band", "sector"), None, None, None),
            P(("band", "sector"), None),
            P(("band", "sector"), None),
            P(),
            P(),
            P(),
            P(),
            P(),
            P(),
            P("band", "sector", None),
        ),
        out_specs=P("band", "sector", None, None),
        check_vma=False,
    )
```

```python
import functools
import math

import jax
import jax.numpy as jnp
from jax import lax
from jax.experimental import pallas as pl
from jax.experimental.pallas import tpu as pltpu
from jax.sharding import PartitionSpec as P

HEADS = 16
HD = 64
GROUP = 4
NGROUP = HEADS // GROUP
GW = GROUP * HD
QUARTER = HD // 4
LISTED = 9
PAIRS = (LISTED + 1) // 2


def whole(shape):
    return pl.BlockSpec(shape, lambda *_: (0,) * len(shape), pipeline_mode=pl.Buffered(1))


def exchange(value, axis, partner):
    count = lax.axis_size(axis)
    return lax.ppermute(value, axis, [(i, partner(i, count)) for i in range(count)])


def added(*terms):
    return sum(term.astype(jnp.float32) for term in terms).astype(jnp.bfloat16)


def place_kernel(start, listing, own, got, out, held, arrived):
    step, tile, chan = out.shape
    items = own.shape[0]
    first = pl.program_id(0) * step

    @pl.when(first == 0)
    def _():
        copies = [
            pltpu.make_async_copy(source, held.at[pl.ds(k * items, items)], arrived.at[k])
            for k, source in enumerate((own, got))
        ]
        for copy in copies:
            copy.start()
        for copy in copies:
            copy.wait()

    def one_slot(k, _):
        def one_item(i, total):
            return total + held[listing[i]].astype(jnp.float32)

        total = jnp.zeros((tile, chan), jnp.float32)
        total = lax.fori_loop(start[first + k], start[first + k + 1], one_item, total)
        out[k] = total.astype(out.dtype)
        return 0

    lax.fori_loop(0, step, one_slot, 0)


def placed(start, listing, own, got):
    slots = start.shape[0] - 1
    items, tile, chan = own.shape
    step = 16
    return pl.pallas_call(
        place_kernel,
        out_shape=jax.ShapeDtypeStruct((slots, tile, chan), own.dtype),
        grid_spec=pltpu.PrefetchScalarGridSpec(
            num_scalar_prefetch=2,
            grid=(slots // step,),
            in_specs=[pl.BlockSpec(memory_space=pl.ANY)] * 2,
            out_specs=pl.BlockSpec((step, tile, chan), lambda i, *_: (i, 0, 0)),
            scratch_shapes=[
                pltpu.VMEM((2 * items, tile, chan), own.dtype),
                pltpu.SemaphoreType.DMA((2,)),
            ],
        ),
        compiler_params=pltpu.CompilerParams(vmem_limit_bytes=24 * 1024 * 1024),
        cost_estimate=pl.CostEstimate(
            flops=0, bytes_accessed=20 * 1024 * 1024, transcendentals=0
        ),
    )(start, listing, own, got)


def in_order(slot, slots):
    items = jnp.arange(slot.shape[0])
    before = (slot[None, :] < slot[:, None]) | (
        (slot[None, :] == slot[:, None]) & (items[None, :] < items[:, None])
    )
    rank = jnp.sum(before.astype(jnp.int32), axis=1)
    listing = jnp.sum(jnp.where(rank[None, :] == items[:, None], items[None, :], 0), axis=1)
    start = jnp.sum((slot[None, :] < jnp.arange(slots + 1)[:, None]).astype(jnp.int32), axis=1)
    return listing.astype(jnp.int32), start


def along_ring(blocks, nz):
    def ahead(step):
        return lambda i, count: (i + 2 * step) % count

    if nz != 4:
        return added(blocks[0], *[exchange(blocks[k], "sector", ahead(k)) for k in range(1, nz)])
    half = blocks[2].shape[-3] // 2
    relay_on = exchange(blocks[2][..., :half, :, :], "sector", ahead(1))
    relay_back = exchange(blocks[2][..., half:, :, :], "sector", ahead(-1))
    on = jnp.concatenate(
        [added(blocks[1][..., :half, :, :], relay_on), blocks[1][..., half:, :, :]], axis=-3
    )
    back = jnp.concatenate(
        [blocks[3][..., :half, :, :], added(blocks[3][..., half:, :, :], relay_back)], axis=-3
    )
    return added(
        blocks[0], exchange(on, "sector", ahead(1)), exchange(back, "sector", ahead(-1))
    )


def other_core(i, count):
    return i ^ 1


def other_x(i, count):
    return i ^ 1


def other_y(i, count):
    return i ^ 2


def reduced_rows(parts, dest, local, trows, tcols, beside):
    nb = lax.axis_size("band")
    ns = lax.axis_size("sector")
    nz = ns // 2
    tile, chan = parts.shape[1:]
    band_at = lax.axis_index("band")
    sect_at = lax.axis_index("sector")
    code = jnp.stack([dest, local])
    code = jnp.concatenate([code, exchange(code, "sector", other_core)], axis=1)
    dest, local = code[0], code[1]
    far_band = (dest // ns) ^ band_at
    far_z = jnp.mod(dest % ns // 2 - sect_at // 2, nz)
    row, col = local // tcols, local % tcols
    z_first = trows // 2
    place = jnp.where(row < z_first, far_z * nb + far_band, far_band * nz + far_z)
    count = nb * nz * tcols
    slot = (row * nb * nz + place) * tcols + col
    slot = jnp.where(dest % 2 == sect_at % 2, slot, trows * count).astype(jnp.int32)
    listing, start = in_order(slot, trows * count)
    got = exchange(parts, "sector", other_core)
    rows = []
    for r in range(trows):
        dense = placed(start[r * count : (r + 1) * count + 1], listing, parts, got)
        if r < z_first:
            dense = dense.reshape(nz, nb, tcols, tile, chan)
            mine = along_ring([dense[k] for k in range(nz)], nz)
            mine = added(
                mine[0],
                exchange(mine[1], "band", other_x),
                exchange(mine[2], "band", other_y),
                exchange(mine[3], "band", lambda i, count: i ^ 3),
            )
        else:
            dense = dense.reshape(nb, nz, tcols, tile, chan)
            half = tcols // 2
            mine = []
            for cols, first, second, order in (
                (slice(0, half), other_x, other_y, (1, 3, 0, 2)),
                (slice(half, tcols), other_y, other_x, (2, 3, 0, 1)),
            ):
                far = jnp.stack([dense[b, :, cols] for b in order[:2]])
                come = exchange(far, "band", first)
                sums = [added(dense[b, :, cols], come[k]) for k, b in enumerate(order[2:])]
                mine.append((sums[0], exchange(sums[1], "band", second)))
            mine, beside = lax.optimization_barrier((mine, beside))
            blocks = [
                jnp.concatenate([added(a[k], b[k]) for a, b in mine], axis=0) for k in range(nz)
            ]
            mine = along_ring(blocks, nz)
        rows.append(mine)
    return rows, beside


def window_rows(rows):
    wide = []
    for row in rows:
        left = exchange(row[-1:], "sector", lambda i, count: (i + 1) % count)
        right = exchange(row[:1], "sector", lambda i, count: (i - 1) % count)
        wide.append(jnp.concatenate([left, row, right], axis=0))
    count = lax.axis_size("band")
    forward = [(i, i + 1) for i in range(count - 1)]
    above = lax.ppermute(wide[-1], "band", forward)
    below = lax.ppermute(wide[0], "band", [(b, a) for a, b in forward])
    return jnp.stack([above, *wide, below])


def rotary_tables(ext_rows, ext_cols, nrows, ncols, tile):
    place = jnp.arange(tile)
    across = (place // 16).astype(jnp.float32)
    along = (place % 16).astype(jnp.float32)
    theta = math.pi * (ext_rows[:, None].astype(jnp.float32) + (across + 0.5) * 16.0 / tile) / nrows
    phi = 2.0 * math.pi * (ext_cols[:, None].astype(jnp.float32) + (along + 0.5) / 16.0) / ncols
    lane = jnp.arange(GROUP * 2 * QUARTER)
    freq = (lane % QUARTER + 1).astype(jnp.float32)
    lon = (lane // QUARTER) % 2 == 1
    lat_angle = theta[:, :, None] * freq
    lon_angle = phi[:, :, None] * freq
    return (
        jnp.where(lon, 0.0, jnp.cos(lat_angle)),
        jnp.where(lon, 0.0, jnp.sin(lat_angle)),
        jnp.where(lon, jnp.cos(lon_angle), 0.0),
        jnp.where(lon, jnp.sin(lon_angle), 0.0),
    )


def pair_order():
    new = jnp.arange(GW)
    second = new // (GW // 2)
    rest = new % (GW // 2)
    old = rest // (2 * QUARTER) * HD + (rest // QUARTER) % 2 * 2 * QUARTER + second * QUARTER
    old = old + rest % QUARTER
    return (jnp.arange(GW)[:, None] == old[None, :]).astype(jnp.bfloat16)


def window_kernel(
    sel,
    cnt,
    npair,
    ext,
    lat_cos,
    lat_sin,
    lon_cos,
    lon_sin,
    gain,
    w_embed,
    w_query,
    w_key,
    w_value,
    w_out,
    order,
    out,
    keys,
    values,
    queries,
    embedded,
    wq_pairs,
    wk_pairs,
    normed,
    attended,
):
    row = pl.program_id(0)
    erows, ecols, tile, chan = ext.shape
    tcols = ecols - 2
    width = w_embed.shape[1]
    f32 = jnp.float32
    bf16 = jnp.bfloat16

    def project_row(r, own):
        for c in range(0, ecols, 2):
            x = ext[r, c : c + 2].reshape(2 * tile, chan)
            emb = jnp.dot(x, w_embed[...], preferred_element_type=f32)
            meansq = jnp.mean(emb * emb, axis=-1, keepdims=True)
            scaled = emb * lax.rsqrt(meansq + 1e-05) * gain[...]
            normed[c * tile : (c + 2) * tile, :] = scaled.astype(bf16)
            if own:
                for k in range(2):
                    if 1 <= c + k <= tcols:
                        embedded[r - 1, c + k - 1] = emb[k * tile : (k + 1) * tile]

        def turn(full, c):
            cosine = lat_cos[r] + lon_cos[c]
            sine = lat_sin[r] + lon_sin[c]
            lower = full[:, : GW // 2]
            upper = full[:, GW // 2 :]
            return jnp.concatenate(
                [lower * cosine - upper * sine, lower * sine + upper * cosine], axis=1
            )

        def one_group(g, _):
            full = jnp.dot(normed[...], wk_pairs[g], preferred_element_type=f32)
            for c in range(ecols):
                keys[r * ecols + c, g] = turn(full[c * tile : (c + 1) * tile], c).astype(bf16)
            cols = pl.ds(pl.multiple_of(g * GW, GW), GW)
            full = jnp.dot(normed[...], w_value[:, cols], preferred_element_type=f32)
            for c in range(ecols):
                values[r * ecols + c, g] = full[c * tile : (c + 1) * tile].astype(bf16)
            if own:
                full = jnp.dot(
                    normed[tile : (tcols + 1) * tile, :], wq_pairs[g], preferred_element_type=f32
                )
                for c in range(tcols):
                    turned = turn(full[c * tile : (c + 1) * tile], c + 1)
                    queries[(r - 1) * tcols + c, g] = (
                        turned * (math.log2(math.e) / math.sqrt(HD))
                    ).astype(bf16)
            return 0

        lax.fori_loop(0, NGROUP, one_group, 0)

    @pl.when(row == 0)
    def _():
        for g in range(NGROUP):
            cols = slice(g * GW, (g + 1) * GW)
            turned = jnp.dot(w_query[:, cols], order[...], preferred_element_type=f32)
            wq_pairs[g] = turned.astype(bf16)
            turned = jnp.dot(w_key[:, cols], order[...], preferred_element_type=f32)
            wk_pairs[g] = turned.astype(bf16)
        project_row(0, False)

        def own_row(r, _):
            project_row(r, True)
            return 0

        lax.fori_loop(1, erows - 1, own_row, 0)
        project_row(erows - 1, False)

    lane = lax.broadcasted_iota(jnp.int32, (tile, GW), 1)
    pair_head = lane % (GW // 2) // (2 * QUARTER)
    value_head = lane // HD

    def one_tile(c, _):
        t = row * tcols + c

        def with_pairs(count):
            def one_group(g, _):
                query = queries[t, g]
                near = jnp.concatenate([keys[sel[t, j], g] for j in range(2 * count)], axis=0)
                held = jnp.concatenate([values[sel[t, j], g] for j in range(2 * count)], axis=0)
                pieces = []
                for first in range(0, GROUP, 2):
                    stacked = jnp.concatenate(
                        [
                            jnp.where(pair_head == h, query, jnp.zeros_like(query))
                            for h in range(first, first + 2)
                        ],
                        axis=0,
                    )
                    scores = lax.dot_general(
                        stacked, near, (((1,), (1,)), ((), ())), preferred_element_type=f32
                    )
                    top = jnp.max(scores, axis=1, keepdims=True)
                    probs = jnp.exp2(scores - top)
                    probs = [
                        probs[:, j * tile : (j + 1) * tile] * cnt[t, j] for j in range(2 * count)
                    ]
                    total = jnp.sum(sum(probs), axis=1, keepdims=True)
                    mixed = jnp.dot(
                        jnp.concatenate(probs, axis=1).astype(bf16), held, preferred_element_type=f32
                    )
                    pieces.append(mixed * (1.0 / total))
                mixed = jnp.concatenate(pieces, axis=0)
                result = mixed[:tile]
                for h in range(1, GROUP):
                    result = jnp.where(value_head == h, mixed[h * tile : (h + 1) * tile], result)
                attended[g, pl.ds(pl.multiple_of(c * tile, tile), tile), :] = result.astype(bf16)
                return 0

            lax.fori_loop(0, NGROUP, one_group, 0, unroll=4)

        for count in range(1, PAIRS + 1):
            pl.when(npair[t] == count)(functools.partial(with_pairs, count))
        return 0

    lax.fori_loop(0, tcols, one_tile, 0)
    for c in range(0, tcols, 2):
        rows = slice(c * tile, (c + 2) * tile)
        together = jnp.concatenate([attended[g, rows, :] for g in range(NGROUP)], axis=1)
        result = jnp.dot(together, w_out[...], preferred_element_type=f32)
        result = result + embedded[row, c : c + 2].reshape(2 * tile, width)
        out[0, c : c + 2] = result.astype(bf16).reshape(2, tile, width)


def window(sel, cnt, npair, operands, trows, tcols):
    ext = operands[0]
    erows, ecols, tile, chan = ext.shape
    width = operands[6].shape[1]
    owned = trows * tcols
    bf16 = jnp.bfloat16
    return pl.pallas_call(
        window_kernel,
        out_shape=jax.ShapeDtypeStruct((trows, tcols, tile, width), bf16),
        grid_spec=pltpu.PrefetchScalarGridSpec(
            num_scalar_prefetch=3,
            grid=(trows,),
            in_specs=[whole(x.shape) for x in operands],
            out_specs=pl.BlockSpec((1, tcols, tile, width), lambda r, *_: (r, 0, 0, 0)),
            scratch_shapes=[
                pltpu.VMEM((erows * ecols, NGROUP, tile, GW), bf16),
                pltpu.VMEM((erows * ecols, NGROUP, tile, GW), bf16),
                pltpu.VMEM((owned, NGROUP, tile, GW), bf16),
                pltpu.VMEM((trows, tcols, tile, width), jnp.float32),
                pltpu.VMEM((NGROUP, width, GW), bf16),
                pltpu.VMEM((NGROUP, width, GW), bf16),
                pltpu.VMEM((ecols * tile, width), bf16),
                pltpu.VMEM((NGROUP, tcols * tile, GW), bf16),
            ],
        ),
        compiler_params=pltpu.CompilerParams(vmem_limit_bytes=62 * 1024 * 1024),
    )(sel, cnt, npair, *operands)


def distinct_tiles(index):
    same = index[:, :, None] == index[:, None, :]
    times = jnp.sum(same, axis=2)
    order = jnp.arange(LISTED)
    new = ~jnp.any(same & (order[None, None, :] < order[None, :, None]), axis=2)
    place = jnp.sum(new[:, None, :] & (order[None, None, :] < order[None, :, None]), axis=2)
    slots = jnp.arange(2 * PAIRS)
    put = new[:, :, None] & (place[:, :, None] == slots[None, None, :])
    found = jnp.any(put, axis=1)
    sel = jnp.where(found, jnp.sum(jnp.where(put, index[:, :, None], 0), axis=1), index[:, :1])
    cnt = jnp.sum(jnp.where(put, times[:, :, None], 0), axis=1).astype(jnp.float32)
    npair = (jnp.sum(new, axis=1) + 1) // 2
    return sel.astype(jnp.int32), cnt, npair.astype(jnp.int32)


def body(
    grid_cells,
    remap_weight,
    remap_dest,
    remap_tile,
    w_embed,
    norm_gain,
    w_query,
    w_key,
    w_value,
    w_out,
    neighbours,
):
    nband = lax.axis_size("band")
    nsect = lax.axis_size("sector")
    blocks, top, rowcells, tile = remap_weight.shape
    chan = grid_cells.shape[2]
    trows, tcols = (neighbours.shape[0], neighbours.shape[1])
    items = blocks * top
    parts = jnp.einsum(
        "rkct,rcf->rktf", remap_weight, grid_cells, preferred_element_type=jnp.float32
    )
    parts = parts.astype(jnp.bfloat16).reshape(items, tile, chan)
    owned = trows * tcols
    band_at = lax.axis_index("band")
    sect_at = lax.axis_index("sector")
    nrows = trows * nband
    ncols = tcols * nsect
    ext_rows = band_at * trows - 1 + jnp.arange(trows + 2)
    ext_cols = jnp.mod(sect_at * tcols - 1 + jnp.arange(tcols + 2), ncols)
    tables = rotary_tables(ext_rows, ext_cols, nrows, ncols, tile)
    local_row = neighbours // ncols - band_at * trows + 1
    local_col = jnp.mod(neighbours % ncols - sect_at * tcols + 1, ncols)
    index = (local_row * (tcols + 2) + local_col).reshape(owned, LISTED)
    beside = (tables, distinct_tiles(index), pair_order())
    dest, local = remap_dest.reshape(-1), remap_tile.reshape(-1)
    rows, beside = reduced_rows(parts, dest, local, trows, tcols, beside)
    tables, (sel, cnt, npair), order = beside
    ext = window_rows(rows)
    operands = (ext, *tables, norm_gain.reshape(1, -1), w_embed)
    operands += (w_query, w_key, w_value, w_out, order)
    return window(sel, cnt, npair, operands, trows, tcols)


def solution(mesh):
    return jax.shard_map(
        body,
        mesh=mesh,
        in_specs=(
            P(("band", "sector"), None, None),
            P(("band", "sector"), None, None, None),
            P(("band", "sector"), None),
            P(("band", "sector"), None),
            P(),
            P(),
            P(),
            P(),
            P(),
            P(),
            P("band", "sector", None),
        ),
        out_specs=P("band", "sector", None, None),
        check_vma=False,
    )
```

```python
import functools
import math

import jax
import jax.numpy as jnp
from jax import lax
from jax.experimental import pallas as pl
from jax.experimental.pallas import tpu as pltpu
from jax.sharding import PartitionSpec as P

HEADS = 16
HD = 64
GROUP = 4
NGROUP = HEADS // GROUP
GW = GROUP * HD
QUARTER = HD // 4
LISTED = 9
EARLY = 4
PAIRS = (LISTED + 1) // 2


def whole(shape):
    return pl.BlockSpec(shape, lambda *_: (0,) * len(shape), pipeline_mode=pl.Buffered(1))


def exchange(value, axis, partner):
    count = lax.axis_size(axis)
    return lax.ppermute(value, axis, [(i, partner(i, count)) for i in range(count)])


def added(*terms):
    return sum(term.astype(jnp.float32) for term in terms).astype(jnp.bfloat16)


def place_kernel(start, listing, *refs):
    sources, (out, held, arrived) = refs[:-3], refs[-3:]
    step, tile, chan = out.shape
    items = sources[0].shape[0]
    first = pl.program_id(0) * step

    @pl.when(first == 0)
    def _():
        copies = [
            pltpu.make_async_copy(source, held.at[pl.ds(k * items, items)], arrived.at[k])
            for k, source in enumerate(sources)
        ]
        for copy in copies:
            copy.start()
        for copy in copies:
            copy.wait()

    def one_slot(k, _):
        def one_item(i, total):
            return total + held[listing[i]].astype(jnp.float32)

        total = jnp.zeros((tile, chan), jnp.float32)
        total = lax.fori_loop(start[first + k], start[first + k + 1], one_item, total)
        out[k] = total.astype(out.dtype)
        return 0

    lax.fori_loop(0, step, one_slot, 0)


def placed(start, listing, sources):
    slots = start.shape[0] - 1
    items, tile, chan = sources[0].shape
    step = 16
    return pl.pallas_call(
        place_kernel,
        out_shape=jax.ShapeDtypeStruct((slots, tile, chan), sources[0].dtype),
        grid_spec=pltpu.PrefetchScalarGridSpec(
            num_scalar_prefetch=2,
            grid=(slots // step,),
            in_specs=[pl.BlockSpec(memory_space=pl.ANY)] * len(sources),
            out_specs=pl.BlockSpec((step, tile, chan), lambda i, *_: (i, 0, 0)),
            scratch_shapes=[
                pltpu.VMEM((len(sources) * items, tile, chan), sources[0].dtype),
                pltpu.SemaphoreType.DMA((len(sources),)),
            ],
        ),
        compiler_params=pltpu.CompilerParams(vmem_limit_bytes=24 * 1024 * 1024),
        cost_estimate=pl.CostEstimate(
            flops=0, bytes_accessed=20 * 1024 * 1024, transcendentals=0
        ),
    )(start, listing, *sources)


def in_order(slot, slots):
    items = jnp.arange(slot.shape[0])
    before = (slot[None, :] < slot[:, None]) | (
        (slot[None, :] == slot[:, None]) & (items[None, :] < items[:, None])
    )
    rank = jnp.sum(before.astype(jnp.int32), axis=1)
    listing = jnp.sum(jnp.where(rank[None, :] == items[:, None], items[None, :], 0), axis=1)
    start = jnp.sum((slot[None, :] < jnp.arange(slots + 1)[:, None]).astype(jnp.int32), axis=1)
    return listing.astype(jnp.int32), start


def along_ring(blocks, nz):
    def ahead(step):
        return lambda i, count: (i + 2 * step) % count

    if nz != 4:
        return added(blocks[0], *[exchange(blocks[k], "sector", ahead(k)) for k in range(1, nz)])
    half = blocks[2].shape[-3] // 2
    relay_on = exchange(blocks[2][..., :half, :, :], "sector", ahead(1))
    relay_back = exchange(blocks[2][..., half:, :, :], "sector", ahead(-1))
    on = jnp.concatenate(
        [added(blocks[1][..., :half, :, :], relay_on), blocks[1][..., half:, :, :]], axis=-3
    )
    back = jnp.concatenate(
        [blocks[3][..., :half, :, :], added(blocks[3][..., half:, :, :], relay_back)], axis=-3
    )
    return added(
        blocks[0], exchange(on, "sector", ahead(1)), exchange(back, "sector", ahead(-1))
    )


def other_core(i, count):
    return i ^ 1


def other_x(i, count):
    return i ^ 1


def other_y(i, count):
    return i ^ 2


def item_order(dest, local, owned):
    nb = lax.axis_size("band")
    ns = lax.axis_size("sector")
    nz = ns // 2
    band_at = lax.axis_index("band")
    sect_at = lax.axis_index("sector")
    code = jnp.stack([dest, local])
    code = jnp.concatenate([code, exchange(code, "sector", other_core)], axis=1)
    dest, local = code[0], code[1]
    far_band = (dest // ns) ^ band_at
    far_z = jnp.mod(dest % ns // 2 - sect_at // 2, nz)
    rest = owned - EARLY
    cut = nb * nz * EARLY
    z_first = (far_z * nb + far_band) * EARLY + local
    band_first = cut + (far_band * nz + far_z) * rest + local - EARLY
    slot = jnp.where(local < EARLY, z_first, band_first)
    slot = jnp.where(dest % 2 == sect_at % 2, slot, nb * nz * owned).astype(jnp.int32)
    listing, start = in_order(slot, nb * nz * owned)
    return listing, start[: cut + 1], start[cut:]


def z_then_band(dense, nz):
    mine = along_ring([dense[k] for k in range(nz)], nz)
    return added(
        mine[0],
        exchange(mine[1], "band", other_x),
        exchange(mine[2], "band", other_y),
        exchange(mine[3], "band", lambda i, count: i ^ 3),
    )


def band_then_z(dense, nz, beside):
    size = dense.shape[2]
    half = size // 2
    mine = []
    for some, first, second, order in (
        (slice(0, half), other_x, other_y, (1, 3, 0, 2)),
        (slice(half, size), other_y, other_x, (2, 3, 0, 1)),
    ):
        far = jnp.stack([dense[b, :, some] for b in order[:2]])
        come = exchange(far, "band", first)
        sums = [added(dense[b, :, some], come[k]) for k, b in enumerate(order[2:])]
        mine.append((sums[0], exchange(sums[1], "band", second)))
    mine, beside = lax.optimization_barrier((mine, beside))
    blocks = [jnp.concatenate([added(a[k], b[k]) for a, b in mine], axis=0) for k in range(nz)]
    return along_ring(blocks, nz), beside


def from_band(row, step):
    count = lax.axis_size("band")
    pairs = [(i, i + step) for i in range(count) if 0 <= i + step < count]
    return lax.ppermute(row, "band", pairs)


def rotary_tables(ext_rows, ext_cols, nrows, ncols, tile):
    place = jnp.arange(tile)
    across = (place // 16).astype(jnp.float32)
    along = (place % 16).astype(jnp.float32)
    theta = math.pi * (ext_rows[:, None].astype(jnp.float32) + (across + 0.5) * 16.0 / tile) / nrows
    phi = 2.0 * math.pi * (ext_cols[:, None].astype(jnp.float32) + (along + 0.5) / 16.0) / ncols
    lane = jnp.arange(GROUP * 2 * QUARTER)
    freq = (lane % QUARTER + 1).astype(jnp.float32)
    lon = (lane // QUARTER) % 2 == 1
    lat_angle = theta[:, :, None] * freq
    lon_angle = phi[:, :, None] * freq
    return (
        jnp.where(lon, 0.0, jnp.cos(lat_angle)),
        jnp.where(lon, 0.0, jnp.sin(lat_angle)),
        jnp.where(lon, jnp.cos(lon_angle), 0.0),
        jnp.where(lon, jnp.sin(lon_angle), 0.0),
    )


def pair_order():
    new = jnp.arange(GW)
    second = new // (GW // 2)
    rest = new % (GW // 2)
    old = rest // (2 * QUARTER) * HD + (rest // QUARTER) % 2 * 2 * QUARTER + second * QUARTER
    old = old + rest % QUARTER
    return (jnp.arange(GW)[:, None] == old[None, :]).astype(jnp.bfloat16)


def norm_row(tiles, gain, w_embed, normed):
    ecols, tile, chan = tiles.shape
    for c in range(0, ecols, 2):
        x = tiles[c : c + 2].reshape(2 * tile, chan)
        emb = jnp.dot(x, w_embed[...], preferred_element_type=jnp.float32)
        meansq = jnp.mean(emb * emb, axis=-1, keepdims=True)
        scaled = emb * lax.rsqrt(meansq + 1e-05) * gain[...]
        normed[c * tile : (c + 2) * tile, :] = scaled.astype(jnp.bfloat16)


def project_group(normed, places, tables, weights, put_key, put_value, put_query):
    wk_pairs, w_value, wq_pairs = weights
    lat_cos, lat_sin, lon_cos, lon_sin = tables
    tile = lat_cos.shape[1]
    normed = normed[: len(places) * tile, :]
    f32 = jnp.float32
    bf16 = jnp.bfloat16

    def turned(full, k):
        r, c = places[k]
        cosine = lat_cos[r] + lon_cos[c]
        sine = lat_sin[r] + lon_sin[c]
        lower = full[k * tile : (k + 1) * tile, : GW // 2]
        upper = full[k * tile : (k + 1) * tile, GW // 2 :]
        return jnp.concatenate(
            [lower * cosine - upper * sine, lower * sine + upper * cosine], axis=1
        )

    full = jnp.dot(normed, wk_pairs, preferred_element_type=f32)
    for k in range(len(places)):
        put_key(k, turned(full, k).astype(bf16))
    full = jnp.dot(normed, w_value, preferred_element_type=f32)
    for k in range(len(places)):
        put_value(k, full[k * tile : (k + 1) * tile].astype(bf16))
    if put_query is not None:
        full = jnp.dot(normed, wq_pairs, preferred_element_type=f32)
        for k in range(len(places)):
            scaled = turned(full, k) * (math.log2(math.e) / math.sqrt(HD))
            put_query(k, scaled.astype(bf16))


def pair_kernel(w_query, w_key, order, wq_pairs, wk_pairs):
    for source, pairs in ((w_query, wq_pairs), (w_key, wk_pairs)):
        turned = jnp.dot(source[...], order[...], preferred_element_type=jnp.float32)
        pairs[0] = turned.astype(jnp.bfloat16)


def in_pairs(w_query, w_key, order):
    width = w_query.shape[0]
    shape = jax.ShapeDtypeStruct((NGROUP, width, GW), jnp.bfloat16)
    cols = pl.BlockSpec((width, GW), lambda g: (0, g))
    group = pl.BlockSpec((1, width, GW), lambda g: (g, 0, 0))
    return pl.pallas_call(
        pair_kernel,
        out_shape=[shape, shape],
        grid=(NGROUP,),
        in_specs=[cols, cols, whole(order.shape)],
        out_specs=[group, group],
        cost_estimate=pl.CostEstimate(
            flops=4 * width * width * GW, bytes_accessed=16 * width * width, transcendentals=0
        ),
    )(w_query, w_key, order)


def row_kernel(*refs):
    tiles, lat_cos, lat_sin, lon_cos, lon_sin, gain, w_embed, wq_pairs, wk_pairs, w_value = refs[:10]
    keys, values, queries, normed = refs[10:]

    @pl.when(pl.program_id(0) == 0)
    def _():
        norm_row(tiles, gain, w_embed, normed)

    def put_key(k, value):
        keys[k, 0] = value

    def put_value(k, value):
        values[k, 0] = value

    def put_query(k, value):
        queries[k, 0] = value

    places = [(0, c) for c in range(tiles.shape[0])]
    weights = (wk_pairs[0], w_value[...], wq_pairs[0])
    tables = (lat_cos, lat_sin, lon_cos, lon_sin)
    project_group(normed, places, tables, weights, put_key, put_value, put_query)


def projected_row(tiles, tables, gain, w_embed, wq_pairs, wk_pairs, w_value):
    count, tile, chan = tiles.shape
    width = w_embed.shape[1]
    bf16 = jnp.bfloat16
    operands = (tiles, *tables, gain, w_embed, wq_pairs, wk_pairs, w_value)
    pairs_spec = pl.BlockSpec((1, width, GW), lambda g: (g, 0, 0))
    in_specs = [whole(x.shape) for x in operands[:-3]]
    in_specs += [pairs_spec, pairs_spec, pl.BlockSpec((width, GW), lambda g: (0, g))]
    return pl.pallas_call(
        row_kernel,
        out_shape=[jax.ShapeDtypeStruct((count, NGROUP, tile, GW), bf16)] * 3,
        grid=(NGROUP,),
        in_specs=in_specs,
        out_specs=[pl.BlockSpec((count, 1, tile, GW), lambda g: (0, g, 0, 0))] * 3,
        scratch_shapes=[pltpu.VMEM((count * tile, width), bf16)],
        compiler_params=pltpu.CompilerParams(vmem_limit_bytes=60 * 1024 * 1024),
        cost_estimate=pl.CostEstimate(
            flops=6 * count * tile * width * width, bytes_accessed=16000000, transcendentals=0
        ),
    )(*operands)


def window_kernel(sel, cnt, npair, *refs):
    above, below, sides, own, lat_cos, lat_sin, lon_cos, lon_sin, gain, w_embed = refs[:10]
    wq_pairs, wk_pairs, w_value = refs[10:13]
    fetched, refs = refs[13:17], refs[17:]
    out, keys, values, queries, normed, attended, w_out_held, sums, arrived = refs
    row = pl.program_id(0)
    trows, tcols, tile, chan = own.shape
    ecols = tcols + 2
    width = w_embed.shape[1]
    f32 = jnp.float32
    bf16 = jnp.bfloat16

    @pl.when(row == 0)
    def _():
        near = pl.ds(trows * ecols + 1, tcols)
        targets = [keys.at[near], values.at[near], queries.at[pl.ds((trows - 1) * tcols, tcols)]]
        copies = [
            pltpu.make_async_copy(source, target, arrived.at[k])
            for k, (source, target) in enumerate(zip(fetched, targets + [w_out_held]))
        ]
        for copy in copies:
            copy.start()
        beside = [(r, c) for r in range(1, trows + 1) for c in (0, ecols - 1)]
        mine = [[(r, c) for c in range(1, ecols - 1)] for r in range(1, trows)]
        for tiles, places in (
            *[(own.at[r], mine[r]) for r in range(trows - 1)],
            (sides, beside),
            (below, [(trows + 1, c) for c in range(ecols)]),
            (above, [(0, c) for c in range(ecols)]),
        ):
            norm_row(tiles, gain, w_embed, normed)

            def one_group(g, _):
                def put_key(k, value):
                    keys[places[k][0] * ecols + places[k][1], g] = value

                def put_value(k, value):
                    values[places[k][0] * ecols + places[k][1], g] = value

                def put_query(k, value):
                    queries[(places[k][0] - 1) * tcols + places[k][1] - 1, g] = value

                cols = pl.ds(pl.multiple_of(g * GW, GW), GW)
                is_own = places in mine
                weights = (wk_pairs[g], w_value[:, cols], wq_pairs[g] if is_own else None)
                tables = (lat_cos, lat_sin, lon_cos, lon_sin)
                last = put_query if is_own else None
                project_group(normed, places, tables, weights, put_key, put_value, last)
                return 0

            lax.fori_loop(0, NGROUP, one_group, 0)
        for copy in copies:
            copy.wait()

    lane = lax.broadcasted_iota(jnp.int32, (tile, GW), 1)
    pair_head = lane % (GW // 2) // (2 * QUARTER)
    first_head = lax.broadcasted_iota(jnp.int32, (tile, tile), 1) < HD
    heads_per = tile // HD

    def stacked_queries(t, g, heads):
        query = queries[t, g]
        return jnp.concatenate(
            [jnp.where(pair_head == h, query, jnp.zeros_like(query)) for h in heads], axis=0
        )

    def put(g, p, c, result):
        rows = pl.ds(pl.multiple_of(c * tile, tile), tile)
        attended[g, rows, p * tile : (p + 1) * tile] = result.astype(bf16)

    def two_heads(mixed, total):
        mixed = mixed / total
        return jnp.where(first_head, mixed[:tile], mixed[tile:])

    def one_tile(c, _):
        t = row * tcols + c

        def with_pairs(count):
            listed = [sel[t, j] for j in range(2 * count)]
            times = [cnt[t, j].astype(bf16) for j in range(2 * count)]
            spread = jnp.concatenate([jnp.full((tile, tile), n, bf16) for n in times], axis=0)
            low, high = sums[0], sums[1]
            for g in range(NGROUP):
                near = jnp.concatenate([keys[j, g] for j in listed], axis=0)
                for p in range(GROUP // heads_per):
                    heads = range(p * heads_per, (p + 1) * heads_per)
                    scores = lax.dot_general(
                        stacked_queries(t, g, heads),
                        near,
                        (((1,), (1,)), ((), ())),
                        preferred_element_type=f32,
                    )
                    lanes = slice(p * tile, (p + 1) * tile)
                    held = jnp.concatenate(
                        [values[j, g, :, lanes] * n for j, n in zip(listed, times)], axis=0
                    )
                    mixed = jnp.dot(
                        jnp.exp2(scores).astype(bf16),
                        jnp.concatenate([held, spread], axis=1),
                        preferred_element_type=f32,
                    )
                    total = mixed[:, tile:]
                    low = jnp.minimum(low, jnp.minimum(total[:tile], total[tile:]))
                    high = jnp.maximum(high, jnp.maximum(total[:tile], total[tile:]))
                    put(g, p, c, two_heads(mixed[:, :tile], total))
            sums[0], sums[1] = low, high

        for count in range(1, PAIRS + 1):
            pl.when(npair[t] == count)(functools.partial(with_pairs, count))
        return 0

    def one_tile_shifted(c, _):
        t = row * tcols + c

        def one_group(g, _):
            near = jnp.concatenate([keys[sel[t, j], g] for j in range(2 * PAIRS)], axis=0)
            for p in range(GROUP // heads_per):
                heads = range(p * heads_per, (p + 1) * heads_per)
                scores = lax.dot_general(
                    stacked_queries(t, g, heads),
                    near,
                    (((1,), (1,)), ((), ())),
                    preferred_element_type=f32,
                )
                probs = jnp.exp2(scores - jnp.max(scores, axis=1, keepdims=True))
                probs = [
                    probs[:, j * tile : (j + 1) * tile] * cnt[t, j] for j in range(2 * PAIRS)
                ]
                held = jnp.concatenate(
                    [values[sel[t, j], g, :, p * tile : (p + 1) * tile] for j in range(2 * PAIRS)],
                    axis=0,
                )
                mixed = jnp.dot(
                    jnp.concatenate(probs, axis=1).astype(bf16), held, preferred_element_type=f32
                )
                put(g, p, c, two_heads(mixed, jnp.sum(sum(probs), axis=1, keepdims=True)))
            return 0

        lax.fori_loop(0, NGROUP, one_group, 0)
        return 0

    sums[0] = jnp.ones((tile, tile), f32)
    sums[1] = jnp.ones((tile, tile), f32)
    lax.fori_loop(0, tcols, one_tile, 0)
    in_range = (jnp.min(sums[0]) >= 2.0**-80) & (jnp.max(sums[1]) <= 2.0**80)

    @pl.when(jnp.logical_not(in_range))
    def _():
        lax.fori_loop(0, tcols, one_tile_shifted, 0)

    for c in range(0, tcols, 2):
        rows = slice(c * tile, (c + 2) * tile)
        together = jnp.concatenate([attended[g, rows, :] for g in range(NGROUP)], axis=1)
        result = jnp.dot(together, w_out_held[...], preferred_element_type=f32)
        tiles = own[row, c : c + 2].reshape(2 * tile, chan)
        result = result + jnp.dot(tiles, w_embed[...], preferred_element_type=f32)
        out[0, c : c + 2] = result.astype(bf16).reshape(2, tile, width)


def window(lists, tiles, tables, gain, w_embed, pairs, w_value, w_out, last):
    trows, tcols, tile, chan = tiles[-1].shape
    ecols = tcols + 2
    width = w_embed.shape[1]
    owned = trows * tcols
    bf16 = jnp.bfloat16
    held = (*tiles, *tables, gain, w_embed, *pairs, w_value)
    fetched = (*last, w_out)
    return pl.pallas_call(
        window_kernel,
        out_shape=jax.ShapeDtypeStruct((trows, tcols, tile, width), bf16),
        grid_spec=pltpu.PrefetchScalarGridSpec(
            num_scalar_prefetch=3,
            grid=(trows,),
            in_specs=[whole(x.shape) for x in held]
            + [pl.BlockSpec(memory_space=pl.ANY)] * len(fetched),
            out_specs=pl.BlockSpec((1, tcols, tile, width), lambda r, *_: (r, 0, 0, 0)),
            scratch_shapes=[
                pltpu.VMEM(((trows + 2) * ecols, NGROUP, tile, GW), bf16),
                pltpu.VMEM(((trows + 2) * ecols, NGROUP, tile, GW), bf16),
                pltpu.VMEM((owned, NGROUP, tile, GW), bf16),
                pltpu.VMEM((ecols * tile, width), bf16),
                pltpu.VMEM((NGROUP, tcols * tile, GW), bf16),
                pltpu.VMEM(w_out.shape, bf16),
                pltpu.VMEM((2, tile, tile), jnp.float32),
                pltpu.SemaphoreType.DMA((len(fetched),)),
            ],
        ),
        compiler_params=pltpu.CompilerParams(vmem_limit_bytes=62 * 1024 * 1024),
    )(*lists, *held, *fetched)


def distinct_tiles(index):
    same = index[:, :, None] == index[:, None, :]
    times = jnp.sum(same, axis=2)
    order = jnp.arange(LISTED)
    new = ~jnp.any(same & (order[None, None, :] < order[None, :, None]), axis=2)
    place = jnp.sum(new[:, None, :] & (order[None, None, :] < order[None, :, None]), axis=2)
    slots = jnp.arange(2 * PAIRS)
    put = new[:, :, None] & (place[:, :, None] == slots[None, None, :])
    found = jnp.any(put, axis=1)
    sel = jnp.where(found, jnp.sum(jnp.where(put, index[:, :, None], 0), axis=1), index[:, :1])
    cnt = jnp.sum(jnp.where(put, times[:, :, None], 0), axis=1).astype(jnp.float32)
    npair = (jnp.sum(new, axis=1) + 1) // 2
    return sel.astype(jnp.int32), cnt, npair.astype(jnp.int32)


def body(
    grid_cells,
    remap_weight,
    remap_dest,
    remap_tile,
    w_embed,
    norm_gain,
    w_query,
    w_key,
    w_value,
    w_out,
    neighbours,
):
    nband = lax.axis_size("band")
    nsect = lax.axis_size("sector")
    blocks, top, rowcells, tile = remap_weight.shape
    chan = grid_cells.shape[2]
    trows, tcols = (neighbours.shape[0], neighbours.shape[1])
    cut = blocks // 2
    parts = []
    for low in (0, cut):
        piece = jnp.einsum(
            "rkct,rcf->rktf",
            remap_weight[low : low + cut],
            grid_cells[low : low + cut],
            preferred_element_type=jnp.float32,
        )
        parts.append(piece.astype(jnp.bfloat16).reshape(cut * top, tile, chan))
    owned = trows * tcols
    band_at = lax.axis_index("band")
    sect_at = lax.axis_index("sector")
    nrows = trows * nband
    ncols = tcols * nsect
    ext_rows = band_at * trows - 1 + jnp.arange(trows + 2)
    ext_cols = jnp.mod(sect_at * tcols - 1 + jnp.arange(tcols + 2), ncols)
    tables = rotary_tables(ext_rows, ext_cols, nrows, ncols, tile)
    local_row = neighbours // ncols - band_at * trows + 1
    local_col = jnp.mod(neighbours % ncols - sect_at * tcols + 1, ncols)
    index = (local_row * (tcols + 2) + local_col).reshape(owned, LISTED)
    dest, local = remap_dest.reshape(-1), remap_tile.reshape(-1)
    listing, first_start, later_start = item_order(dest, local, owned)
    parts += [exchange(piece, "sector", other_core) for piece in parts]
    nz = nsect // 2
    block = (tile, chan)
    gain = norm_gain.reshape(1, -1)
    beside = (tables, distinct_tiles(index), in_pairs(w_query, w_key, pair_order()))
    z_first = placed(first_start, listing, parts).reshape(nz, nband, EARLY, *block)
    ends = z_then_band(z_first, nz)
    band_first = placed(later_start, listing, parts)
    band_first = band_first.reshape(nband, nz, owned - EARLY, *block)
    later, beside = band_then_z(band_first, nz, beside)
    tables, lists, pairs = beside
    own = jnp.concatenate([ends, later], axis=0)
    own = own.reshape(trows, tcols, *block)

    left = exchange(own[:, -1:], "sector", lambda i, count: (i + 1) % count)
    right = exchange(own[:, :1], "sector", lambda i, count: (i - 1) % count)
    left, right, held_back = lax.optimization_barrier((left, right, own[-1]))
    above = from_band(jnp.concatenate([left[-1], own[-1], right[-1]], axis=0), 1)
    below = from_band(jnp.concatenate([left[0], own[0], right[0]], axis=0), -1)
    lat = (tables[0][trows : trows + 1], tables[1][trows : trows + 1])
    lon = (tables[2][1 : tcols + 1], tables[3][1 : tcols + 1])
    last = projected_row(held_back, (*lat, *lon), gain, w_embed, *pairs, w_value)
    sides = jnp.concatenate([left, right], axis=1)
    tiles = (above, below, sides.reshape(2 * trows, *block), own)
    return window(lists, tiles, tables, gain, w_embed, pairs, w_value, w_out, last)


def solution(mesh):
    return jax.shard_map(
        body,
        mesh=mesh,
        in_specs=(
            P(("band", "sector"), None, None),
            P(("band", "sector"), None, None, None),
            P(("band", "sector"), None),
            P(("band", "sector"), None),
            P(),
            P(),
            P(),
            P(),
            P(),
            P(),
            P("band", "sector", None),
        ),
        out_specs=P("band", "sector", None, None),
        check_vma=False,
    )
```

```python
import functools
import math

import jax
import jax.numpy as jnp
from jax import lax
from jax.experimental import pallas as pl
from jax.experimental.pallas import tpu as pltpu
from jax.sharding import PartitionSpec as P

HEADS = 16
HD = 64
GROUP = 4
NGROUP = HEADS // GROUP
GW = GROUP * HD
QUARTER = HD // 4
LISTED = 9
EARLY = 4
PAIRS = (LISTED + 1) // 2


def whole(shape):
    return pl.BlockSpec(shape, lambda *_: (0,) * len(shape), pipeline_mode=pl.Buffered(1))


def exchange(value, axis, partner):
    count = lax.axis_size(axis)
    return lax.ppermute(value, axis, [(i, partner(i, count)) for i in range(count)])


def added(*terms):
    return sum(term.astype(jnp.float32) for term in terms).astype(jnp.bfloat16)


def place_kernel(start, listing, *refs):
    sources, (out, held, arrived) = refs[:-3], refs[-3:]
    step, tile, chan = out.shape
    items = sources[0].shape[0]
    first = pl.program_id(0) * step

    @pl.when(first == 0)
    def _():
        copies = [
            pltpu.make_async_copy(source, held.at[pl.ds(k * items, items)], arrived.at[k])
            for k, source in enumerate(sources)
        ]
        for copy in copies:
            copy.start()
        for copy in copies:
            copy.wait()

    def one_slot(k, _):
        def one_item(i, total):
            return total + held[listing[i]].astype(jnp.float32)

        total = jnp.zeros((tile, chan), jnp.float32)
        total = lax.fori_loop(start[first + k], start[first + k + 1], one_item, total)
        out[k] = total.astype(out.dtype)
        return 0

    lax.fori_loop(0, step, one_slot, 0)


def placed(start, listing, sources):
    slots = start.shape[0] - 1
    items, tile, chan = sources[0].shape
    step = 16
    return pl.pallas_call(
        place_kernel,
        out_shape=jax.ShapeDtypeStruct((slots, tile, chan), sources[0].dtype),
        grid_spec=pltpu.PrefetchScalarGridSpec(
            num_scalar_prefetch=2,
            grid=(slots // step,),
            in_specs=[pl.BlockSpec(memory_space=pl.ANY)] * len(sources),
            out_specs=pl.BlockSpec((step, tile, chan), lambda i, *_: (i, 0, 0)),
            scratch_shapes=[
                pltpu.VMEM((len(sources) * items, tile, chan), sources[0].dtype),
                pltpu.SemaphoreType.DMA((len(sources),)),
            ],
        ),
        compiler_params=pltpu.CompilerParams(vmem_limit_bytes=24 * 1024 * 1024),
        cost_estimate=pl.CostEstimate(
            flops=0, bytes_accessed=20 * 1024 * 1024, transcendentals=0
        ),
    )(start, listing, *sources)


def in_order(slot, slots):
    items = jnp.arange(slot.shape[0])
    before = (slot[None, :] < slot[:, None]) | (
        (slot[None, :] == slot[:, None]) & (items[None, :] < items[:, None])
    )
    rank = jnp.sum(before.astype(jnp.int32), axis=1)
    listing = jnp.sum(jnp.where(rank[None, :] == items[:, None], items[None, :], 0), axis=1)
    start = jnp.sum((slot[None, :] < jnp.arange(slots + 1)[:, None]).astype(jnp.int32), axis=1)
    return listing.astype(jnp.int32), start


def along_ring(blocks, nz):
    def ahead(step):
        return lambda i, count: (i + 2 * step) % count

    if nz != 4:
        return added(blocks[0], *[exchange(blocks[k], "sector", ahead(k)) for k in range(1, nz)])
    half = blocks[2].shape[-3] // 2
    relay_on = exchange(blocks[2][..., :half, :, :], "sector", ahead(1))
    relay_back = exchange(blocks[2][..., half:, :, :], "sector", ahead(-1))
    on = jnp.concatenate(
        [added(blocks[1][..., :half, :, :], relay_on), blocks[1][..., half:, :, :]], axis=-3
    )
    back = jnp.concatenate(
        [blocks[3][..., :half, :, :], added(blocks[3][..., half:, :, :], relay_back)], axis=-3
    )
    return added(
        blocks[0], exchange(on, "sector", ahead(1)), exchange(back, "sector", ahead(-1))
    )


def other_core(i, count):
    return i ^ 1


def other_x(i, count):
    return i ^ 1


def other_y(i, count):
    return i ^ 2


def item_order(dest, local, owned):
    nb = lax.axis_size("band")
    ns = lax.axis_size("sector")
    nz = ns // 2
    band_at = lax.axis_index("band")
    sect_at = lax.axis_index("sector")
    code = jnp.stack([dest, local])
    code = jnp.concatenate([code, exchange(code, "sector", other_core)], axis=1)
    dest, local = code[0], code[1]
    far_band = (dest // ns) ^ band_at
    far_z = jnp.mod(dest % ns // 2 - sect_at // 2, nz)
    rest = owned - EARLY
    cut = nb * nz * EARLY
    z_first = (far_z * nb + far_band) * EARLY + local
    band_first = cut + (far_band * nz + far_z) * rest + local - EARLY
    slot = jnp.where(local < EARLY, z_first, band_first)
    slot = jnp.where(dest % 2 == sect_at % 2, slot, nb * nz * owned).astype(jnp.int32)
    listing, start = in_order(slot, nb * nz * owned)
    return listing, start[: cut + 1], start[cut:]


def z_then_band(dense, nz):
    mine = along_ring([dense[k] for k in range(nz)], nz)
    return added(
        mine[0],
        exchange(mine[1], "band", other_x),
        exchange(mine[2], "band", other_y),
        exchange(mine[3], "band", lambda i, count: i ^ 3),
    )


def band_then_z(dense, nz, beside):
    size = dense.shape[2]
    half = size // 2
    mine = []
    for some, first, second, order in (
        (slice(0, half), other_x, other_y, (1, 3, 0, 2)),
        (slice(half, size), other_y, other_x, (2, 3, 0, 1)),
    ):
        far = jnp.stack([dense[b, :, some] for b in order[:2]])
        come = exchange(far, "band", first)
        sums = [added(dense[b, :, some], come[k]) for k, b in enumerate(order[2:])]
        mine.append((sums[0], exchange(sums[1], "band", second)))
    mine, beside = lax.optimization_barrier((mine, beside))
    blocks = [jnp.concatenate([added(a[k], b[k]) for a, b in mine], axis=0) for k in range(nz)]
    return along_ring(blocks, nz), beside


def from_band(row, step):
    count = lax.axis_size("band")
    pairs = [(i, i + step) for i in range(count) if 0 <= i + step < count]
    return lax.ppermute(row, "band", pairs)


def rotary_tables(ext_rows, ext_cols, nrows, ncols, tile):
    place = jnp.arange(tile)
    across = (place // 16).astype(jnp.float32)
    along = (place % 16).astype(jnp.float32)
    theta = math.pi * (ext_rows[:, None].astype(jnp.float32) + (across + 0.5) * 16.0 / tile) / nrows
    phi = 2.0 * math.pi * (ext_cols[:, None].astype(jnp.float32) + (along + 0.5) / 16.0) / ncols
    lane = jnp.arange(GROUP * 2 * QUARTER)
    freq = (lane % QUARTER + 1).astype(jnp.float32)
    lon = (lane // QUARTER) % 2 == 1
    lat_angle = theta[:, :, None] * freq
    lon_angle = phi[:, :, None] * freq
    return (
        jnp.where(lon, 0.0, jnp.cos(lat_angle)),
        jnp.where(lon, 0.0, jnp.sin(lat_angle)),
        jnp.where(lon, jnp.cos(lon_angle), 0.0),
        jnp.where(lon, jnp.sin(lon_angle), 0.0),
    )


def pair_order():
    new = jnp.arange(GW)
    second = new // (GW // 2)
    rest = new % (GW // 2)
    old = rest // (2 * QUARTER) * HD + (rest // QUARTER) % 2 * 2 * QUARTER + second * QUARTER
    old = old + rest % QUARTER
    return (jnp.arange(GW)[:, None] == old[None, :]).astype(jnp.bfloat16)


def norm_row(tiles, gain, w_embed, normed):
    ecols, tile, chan = tiles.shape
    for c in range(0, ecols, 2):
        x = tiles[c : c + 2].reshape(2 * tile, chan)
        emb = jnp.dot(x, w_embed[...], preferred_element_type=jnp.float32)
        meansq = jnp.mean(emb * emb, axis=-1, keepdims=True)
        scaled = emb * lax.rsqrt(meansq + 1e-05) * gain[...]
        normed[c * tile : (c + 2) * tile, :] = scaled.astype(jnp.bfloat16)


def project_group(normed, places, tables, weights, put_key, put_value, put_query):
    wk_pairs, w_value, wq_pairs = weights
    lat_cos, lat_sin, lon_cos, lon_sin = tables
    tile = lat_cos.shape[1]
    normed = normed[: len(places) * tile, :]
    f32 = jnp.float32
    bf16 = jnp.bfloat16

    def turned(full, k):
        r, c = places[k]
        cosine = lat_cos[r] + lon_cos[c]
        sine = lat_sin[r] + lon_sin[c]
        lower = full[k * tile : (k + 1) * tile, : GW // 2]
        upper = full[k * tile : (k + 1) * tile, GW // 2 :]
        return jnp.concatenate(
            [lower * cosine - upper * sine, lower * sine + upper * cosine], axis=1
        )

    full = jnp.dot(normed, wk_pairs, preferred_element_type=f32)
    for k in range(len(places)):
        put_key(k, turned(full, k).astype(bf16))
    full = jnp.dot(normed, w_value, preferred_element_type=f32)
    for k in range(len(places)):
        put_value(k, full[k * tile : (k + 1) * tile].astype(bf16))
    if put_query is not None:
        full = jnp.dot(normed, wq_pairs, preferred_element_type=f32)
        for k in range(len(places)):
            scaled = turned(full, k) * (math.log2(math.e) / math.sqrt(HD))
            put_query(k, scaled.astype(bf16))


def pair_kernel(w_query, w_key, order, wq_pairs, wk_pairs):
    for source, pairs in ((w_query, wq_pairs), (w_key, wk_pairs)):
        turned = jnp.dot(source[...], order[...], preferred_element_type=jnp.float32)
        pairs[0] = turned.astype(jnp.bfloat16)


def in_pairs(w_query, w_key, order):
    width = w_query.shape[0]
    shape = jax.ShapeDtypeStruct((NGROUP, width, GW), jnp.bfloat16)
    cols = pl.BlockSpec((width, GW), lambda g: (0, g))
    group = pl.BlockSpec((1, width, GW), lambda g: (g, 0, 0))
    return pl.pallas_call(
        pair_kernel,
        out_shape=[shape, shape],
        grid=(NGROUP,),
        in_specs=[cols, cols, whole(order.shape)],
        out_specs=[group, group],
        cost_estimate=pl.CostEstimate(
            flops=4 * width * width * GW, bytes_accessed=16 * width * width, transcendentals=0
        ),
    )(w_query, w_key, order)


def row_kernel(*refs):
    tiles, lat_cos, lat_sin, lon_cos, lon_sin, gain, w_embed, wq_pairs, wk_pairs, w_value = refs[:10]
    keys, values, queries, normed = refs[10:]

    @pl.when(pl.program_id(0) == 0)
    def _():
        norm_row(tiles, gain, w_embed, normed)

    def put_key(k, value):
        keys[k, 0] = value

    def put_value(k, value):
        values[k, 0] = value

    def put_query(k, value):
        queries[k, 0] = value

    tcols = lon_cos.shape[0]
    places = [(k // tcols, k % tcols) for k in range(tiles.shape[0])]
    weights = (wk_pairs[0], w_value[...], wq_pairs[0])
    tables = (lat_cos, lat_sin, lon_cos, lon_sin)
    project_group(normed, places, tables, weights, put_key, put_value, put_query)


def projected_row(tiles, tables, gain, w_embed, wq_pairs, wk_pairs, w_value):
    count, tile, chan = tiles.shape
    width = w_embed.shape[1]
    bf16 = jnp.bfloat16
    operands = (tiles, *tables, gain, w_embed, wq_pairs, wk_pairs, w_value)
    pairs_spec = pl.BlockSpec((1, width, GW), lambda g: (g, 0, 0))
    in_specs = [whole(x.shape) for x in operands[:-3]]
    in_specs += [pairs_spec, pairs_spec, pl.BlockSpec((width, GW), lambda g: (0, g))]
    return pl.pallas_call(
        row_kernel,
        out_shape=[jax.ShapeDtypeStruct((count, NGROUP, tile, GW), bf16)] * 3,
        grid=(NGROUP,),
        in_specs=in_specs,
        out_specs=[pl.BlockSpec((count, 1, tile, GW), lambda g: (0, g, 0, 0))] * 3,
        scratch_shapes=[pltpu.VMEM((count * tile, width), bf16)],
        compiler_params=pltpu.CompilerParams(vmem_limit_bytes=60 * 1024 * 1024),
        cost_estimate=pl.CostEstimate(
            flops=6 * count * tile * width * width, bytes_accessed=16000000, transcendentals=0
        ),
    )(*operands)


def window_kernel(sel, cnt, npair, *refs):
    above, below, sides, own, lat_cos, lat_sin, lon_cos, lon_sin, gain, w_embed = refs[:10]
    wk_pairs, w_value = refs[10:12]
    fetched, refs = refs[12:16], refs[16:]
    out, keys, values, queries, normed, attended, w_out_held, sums, arrived = refs
    row = pl.program_id(0)
    trows, tcols, tile, chan = own.shape
    ecols = tcols + 2
    width = w_embed.shape[1]
    f32 = jnp.float32
    bf16 = jnp.bfloat16

    @pl.when(row == 0)
    def _():
        sources, targets = [], []
        for r in range(trows):
            near = pl.ds((r + 1) * ecols + 1, tcols)
            mine = pl.ds(r * tcols, tcols)
            sources += [x.at[mine] for x in fetched[:3]]
            targets += [keys.at[near], values.at[near], queries.at[mine]]
        sources.append(fetched[3])
        copies = [
            pltpu.make_async_copy(source, target, arrived.at[k])
            for k, (source, target) in enumerate(zip(sources, targets + [w_out_held]))
        ]
        for copy in copies:
            copy.start()
        beside = [(r, c) for r in range(1, trows + 1) for c in (0, ecols - 1)]
        for tiles, places in (
            (sides, beside),
            (below, [(trows + 1, c) for c in range(ecols)]),
            (above, [(0, c) for c in range(ecols)]),
        ):
            norm_row(tiles, gain, w_embed, normed)

            def one_group(g, _):
                def put_key(k, value):
                    keys[places[k][0] * ecols + places[k][1], g] = value

                def put_value(k, value):
                    values[places[k][0] * ecols + places[k][1], g] = value

                cols = pl.ds(pl.multiple_of(g * GW, GW), GW)
                weights = (wk_pairs[g], w_value[:, cols], None)
                tables = (lat_cos, lat_sin, lon_cos, lon_sin)
                project_group(normed, places, tables, weights, put_key, put_value, None)
                return 0

            lax.fori_loop(0, NGROUP, one_group, 0)
        for copy in copies:
            copy.wait()

    lane = lax.broadcasted_iota(jnp.int32, (tile, GW), 1)
    pair_head = lane % (GW // 2) // (2 * QUARTER)
    first_head = lax.broadcasted_iota(jnp.int32, (tile, tile), 1) < HD
    heads_per = tile // HD

    def stacked_queries(t, g, heads):
        query = queries[t, g]
        return jnp.concatenate(
            [jnp.where(pair_head == h, query, jnp.zeros_like(query)) for h in heads], axis=0
        )

    def put(g, p, c, result):
        rows = pl.ds(pl.multiple_of(c * tile, tile), tile)
        attended[g, rows, p * tile : (p + 1) * tile] = result.astype(bf16)

    def two_heads(mixed, total):
        mixed = jnp.where(first_head, mixed[:tile], mixed[tile:])
        return mixed / jnp.where(first_head, total[:tile], total[tile:])

    def one_tile(c, _):
        t = row * tcols + c

        def with_pairs(count):
            listed = [sel[t, j] for j in range(2 * count)]
            times = [cnt[t, j].astype(bf16) for j in range(2 * count)]
            spread = jnp.concatenate([jnp.full((tile, tile), n, bf16) for n in times], axis=0)
            low, high = sums[0], sums[1]
            for g in range(NGROUP):
                near = jnp.concatenate([keys[j, g] for j in listed], axis=0)
                for p in range(GROUP // heads_per):
                    heads = range(p * heads_per, (p + 1) * heads_per)
                    scores = lax.dot_general(
                        stacked_queries(t, g, heads),
                        near,
                        (((1,), (1,)), ((), ())),
                        preferred_element_type=f32,
                    )
                    lanes = slice(p * tile, (p + 1) * tile)
                    held = jnp.concatenate(
                        [values[j, g, :, lanes] * n for j, n in zip(listed, times)], axis=0
                    )
                    mixed = jnp.dot(
                        jnp.exp2(scores).astype(bf16),
                        jnp.concatenate([held, spread], axis=1),
                        preferred_element_type=f32,
                    )
                    total = mixed[:, tile:]
                    low = jnp.minimum(low, jnp.minimum(total[:tile], total[tile:]))
                    high = jnp.maximum(high, jnp.maximum(total[:tile], total[tile:]))
                    put(g, p, c, two_heads(mixed[:, :tile], total))
            sums[0], sums[1] = low, high

        for count in range(1, PAIRS + 1):
            pl.when(npair[t] == count)(functools.partial(with_pairs, count))
        return 0

    def one_tile_shifted(c, _):
        t = row * tcols + c

        def one_group(g, _):
            near = jnp.concatenate([keys[sel[t, j], g] for j in range(2 * PAIRS)], axis=0)
            for p in range(GROUP // heads_per):
                heads = range(p * heads_per, (p + 1) * heads_per)
                scores = lax.dot_general(
                    stacked_queries(t, g, heads),
                    near,
                    (((1,), (1,)), ((), ())),
                    preferred_element_type=f32,
                )
                probs = jnp.exp2(scores - jnp.max(scores, axis=1, keepdims=True))
                probs = [
                    probs[:, j * tile : (j + 1) * tile] * cnt[t, j] for j in range(2 * PAIRS)
                ]
                held = jnp.concatenate(
                    [values[sel[t, j], g, :, p * tile : (p + 1) * tile] for j in range(2 * PAIRS)],
                    axis=0,
                )
                mixed = jnp.dot(
                    jnp.concatenate(probs, axis=1).astype(bf16), held, preferred_element_type=f32
                )
                put(g, p, c, two_heads(mixed, jnp.sum(sum(probs), axis=1, keepdims=True)))
            return 0

        lax.fori_loop(0, NGROUP, one_group, 0)
        return 0

    sums[0] = jnp.ones((tile, tile), f32)
    sums[1] = jnp.ones((tile, tile), f32)
    lax.fori_loop(0, tcols, one_tile, 0)
    in_range = (jnp.min(sums[0]) >= 2.0**-80) & (jnp.max(sums[1]) <= 2.0**80)

    @pl.when(jnp.logical_not(in_range))
    def _():
        lax.fori_loop(0, tcols, one_tile_shifted, 0)

    for c in range(0, tcols, 2):
        rows = slice(c * tile, (c + 2) * tile)
        together = jnp.concatenate([attended[g, rows, :] for g in range(NGROUP)], axis=1)
        result = jnp.dot(together, w_out_held[...], preferred_element_type=f32)
        tiles = own[row, c : c + 2].reshape(2 * tile, chan)
        result = result + jnp.dot(tiles, w_embed[...], preferred_element_type=f32)
        out[0, c : c + 2] = result.astype(bf16).reshape(2, tile, width)


def window(lists, tiles, tables, gain, w_embed, pairs, w_value, w_out, last):
    trows, tcols, tile, chan = tiles[-1].shape
    ecols = tcols + 2
    width = w_embed.shape[1]
    owned = trows * tcols
    bf16 = jnp.bfloat16
    held = (*tiles, *tables, gain, w_embed, pairs[1], w_value)
    fetched = (*last, w_out)
    return pl.pallas_call(
        window_kernel,
        out_shape=jax.ShapeDtypeStruct((trows, tcols, tile, width), bf16),
        grid_spec=pltpu.PrefetchScalarGridSpec(
            num_scalar_prefetch=3,
            grid=(trows,),
            in_specs=[whole(x.shape) for x in held]
            + [pl.BlockSpec(memory_space=pl.ANY)] * len(fetched),
            out_specs=pl.BlockSpec((1, tcols, tile, width), lambda r, *_: (r, 0, 0, 0)),
            scratch_shapes=[
                pltpu.VMEM(((trows + 2) * ecols, NGROUP, tile, GW), bf16),
                pltpu.VMEM(((trows + 2) * ecols, NGROUP, tile, GW), bf16),
                pltpu.VMEM((owned, NGROUP, tile, GW), bf16),
                pltpu.VMEM((ecols * tile, width), bf16),
                pltpu.VMEM((NGROUP, tcols * tile, GW), bf16),
                pltpu.VMEM(w_out.shape, bf16),
                pltpu.VMEM((2, tile, tile), jnp.float32),
                pltpu.SemaphoreType.DMA((3 * trows + 1,)),
            ],
        ),
        compiler_params=pltpu.CompilerParams(vmem_limit_bytes=62 * 1024 * 1024),
    )(*lists, *held, *fetched)


def distinct_tiles(index):
    same = index[:, :, None] == index[:, None, :]
    times = jnp.sum(same, axis=2)
    order = jnp.arange(LISTED)
    new = ~jnp.any(same & (order[None, None, :] < order[None, :, None]), axis=2)
    place = jnp.sum(new[:, None, :] & (order[None, None, :] < order[None, :, None]), axis=2)
    slots = jnp.arange(2 * PAIRS)
    put = new[:, :, None] & (place[:, :, None] == slots[None, None, :])
    found = jnp.any(put, axis=1)
    sel = jnp.where(found, jnp.sum(jnp.where(put, index[:, :, None], 0), axis=1), index[:, :1])
    cnt = jnp.sum(jnp.where(put, times[:, :, None], 0), axis=1).astype(jnp.float32)
    npair = (jnp.sum(new, axis=1) + 1) // 2
    return sel.astype(jnp.int32), cnt, npair.astype(jnp.int32)


def body(
    grid_cells,
    remap_weight,
    remap_dest,
    remap_tile,
    w_embed,
    norm_gain,
    w_query,
    w_key,
    w_value,
    w_out,
    neighbours,
):
    nband = lax.axis_size("band")
    nsect = lax.axis_size("sector")
    blocks, top, rowcells, tile = remap_weight.shape
    chan = grid_cells.shape[2]
    trows, tcols = (neighbours.shape[0], neighbours.shape[1])
    cut = blocks // 2
    parts = []
    for low in (0, cut):
        piece = jnp.einsum(
            "rkct,rcf->rktf",
            remap_weight[low : low + cut],
            grid_cells[low : low + cut],
            preferred_element_type=jnp.float32,
        )
        parts.append(piece.astype(jnp.bfloat16).reshape(cut * top, tile, chan))
    owned = trows * tcols
    band_at = lax.axis_index("band")
    sect_at = lax.axis_index("sector")
    nrows = trows * nband
    ncols = tcols * nsect
    ext_rows = band_at * trows - 1 + jnp.arange(trows + 2)
    ext_cols = jnp.mod(sect_at * tcols - 1 + jnp.arange(tcols + 2), ncols)
    local_row = neighbours // ncols - band_at * trows + 1
    local_col = jnp.mod(neighbours % ncols - sect_at * tcols + 1, ncols)
    index = (local_row * (tcols + 2) + local_col).reshape(owned, LISTED)
    dest, local = remap_dest.reshape(-1), remap_tile.reshape(-1)
    listing, first_start, later_start = item_order(dest, local, owned)
    parts += [exchange(piece, "sector", other_core) for piece in parts]
    nz = nsect // 2
    block = (tile, chan)
    gain = norm_gain.reshape(1, -1)
    tables = rotary_tables(ext_rows, ext_cols, nrows, ncols, tile)
    beside = (tables, distinct_tiles(index), in_pairs(w_query, w_key, pair_order()))
    z_first = placed(first_start, listing, parts)
    ends = z_then_band(z_first.reshape(nz, nband, EARLY, *block), nz)
    band_first = placed(later_start, listing, parts)
    band_first = band_first.reshape(nband, nz, owned - EARLY, *block)
    later, beside = band_then_z(band_first, nz, beside)
    tables, lists, pairs = beside
    own = jnp.concatenate([ends, later], axis=0)
    own = own.reshape(trows, tcols, *block)

    left = exchange(own[:, -1:], "sector", lambda i, count: (i + 1) % count)
    right = exchange(own[:, :1], "sector", lambda i, count: (i - 1) % count)
    left, right, held_back = lax.optimization_barrier((left, right, own))
    above = from_band(jnp.concatenate([left[-1], own[-1], right[-1]], axis=0), 1)
    below = from_band(jnp.concatenate([left[0], own[0], right[0]], axis=0), -1)
    lat = (tables[0][1 : trows + 1], tables[1][1 : trows + 1])
    lon = (tables[2][1 : tcols + 1], tables[3][1 : tcols + 1])
    held_back = held_back.reshape(owned, *block)
    last = projected_row(held_back, (*lat, *lon), gain, w_embed, *pairs, w_value)
    sides = jnp.concatenate([left, right], axis=1)
    tiles = (above, below, sides.reshape(2 * trows, *block), own)
    return window(lists, tiles, tables, gain, w_embed, pairs, w_value, w_out, last)


def solution(mesh):
    return jax.shard_map(
        body,
        mesh=mesh,
        in_specs=(
            P(("band", "sector"), None, None),
            P(("band", "sector"), None, None, None),
            P(("band", "sector"), None),
            P(("band", "sector"), None),
            P(),
            P(),
            P(),
            P(),
            P(),
            P(),
            P("band", "sector", None),
        ),
        out_specs=P("band", "sector", None, None),
        check_vma=False,
    )
```
